256 devices in a mesh: lat: 32 (over x_lo, z, core), lon: 8 (over x_hi, y).
Axes of the slice: x: 4 (x_hi: 2, x_lo: 2; x = x_hi * 2 + x_lo), y: 4, z: 8, core: 2. Of those that a mesh axis runs over, the one named last changes fastest.
Arguments:
- ocean_state: bfloat16 [256, 1024, 384], P('lat', 'lon'), may hold values from -6 to 6
- kernel: float32 [49, 384], replicated, may hold values from -0.875 to 0.875
- norm_gain: float32 [384], replicated, may hold values from 0.5 to 1.5
- weight_in: bfloat16 [384, 1536], P('lat'), may hold values from -0.3125 to 0.3125
- weight_out: bfloat16 [1536, 384], P('lat'), may hold values from -0.15625 to 0.15625
- layer_scale: float32 [384], replicated, may hold values from 0.5 to 1.5
- cotangent: bfloat16 [256, 1024, 384], P('lat', 'lon'), may hold values from -6 to 6
- tile_list: int32 [32, 8, 6], P('lat', 'lon'), may hold values from 0 to 7, as said below
- ocean_count: int32 [32, 8], P('lat', 'lon'), may hold values from 1 to 6, as said below
Outputs:
- new_state: bfloat16 [256, 1024, 384], P('lat', 'lon')
- grad_state: bfloat16 [256, 1024, 384], P('lat', 'lon')
- grad_weight_in: float32 [384, 1536], P('lat')
- grad_weight_out: float32 [1536, 384], P('lat')
- grad_kernel: float32 [49, 384], replicated
The draws below stay inside these ranges and needn't reach their ends.
Inputs may be any that keep to these rules, and one draw needn't show every extreme that they name: `tile_list`: for each device, 6 distinct tile numbers of its own block; the first ocean_count of them are its ocean tiles, the others are land tiles. `ocean_count`: ocean tiles of each device; some device has exactly 6.
All inputs are finite; a program needn't handle non-finite values.
Results may differ from the reference program's by a relative error of at most 0.0062.
Values may be sent and summed in bfloat16 or wider, within the bound.
A program may use at most 128 MiB of HBM per device.

```python
import math
import jax
import jax.numpy as jnp
from jax import lax

C = 384
FF = 1536
TAPS = 7
TILE = 128
ROWS_DEV = 8
REACH = 3
TILES_ROW = 1
TILES_DEV = 8
OCEAN_MAX = 6
LAT_DEVS = 32
LON_DEVS = 8
NLAT = 256
NLON = 1024


def draw_ocean_count(key, part):
    key = jax.random.fold_in(key, 3)
    loads = jax.random.randint(jax.random.fold_in(key, 11), (LAT_DEVS, LON_DEVS), 0, OCEAN_MAX)
    counts = 1 + loads * loads // (OCEAN_MAX - 1)
    full_at = jax.random.randint(jax.random.fold_in(key, 12), (), 0, LAT_DEVS * LON_DEVS)
    places = jnp.arange(LAT_DEVS * LON_DEVS, dtype=jnp.int32).reshape(LAT_DEVS, LON_DEVS)
    return jnp.where(places == full_at, OCEAN_MAX, counts).astype(jnp.int32)


def draw_tile_list(key, part):
    key = jax.random.fold_in(key, 5)
    scores = jax.random.randint(key, (LAT_DEVS, LON_DEVS, TILES_DEV), 0, 1 << 20)
    scores = scores * TILES_DEV + jnp.arange(TILES_DEV, dtype=jnp.int32)
    order = jnp.argsort(scores, axis=-1, stable=True)
    return order[..., :OCEAN_MAX].astype(jnp.int32)


def block_levels(stream_key, extent, cuts, smallest, largest):
    factor_of = 1.0
    for dim, shards_of in cuts:
        heights = jax.random.uniform(jax.random.fold_in(jax.random.fold_in(stream_key, 6), dim), (shards_of,), jnp.float32, smallest / len(cuts), largest / len(cuts))
        factor_of = factor_of * jnp.repeat(jnp.exp(heights), extent[dim] // shards_of).reshape((-1,) + (1,) * (len(extent) - 1 - dim))
    return factor_of


def noise(key, shape, deviation, bound, shards=(), kind=jnp.bfloat16):
    values = deviation * jax.random.normal(key, shape, jnp.float32)
    if shards:
        values = values * block_levels(key, shape, shards, -0.22, 0.18)
    return jnp.clip(values, -bound, bound).astype(kind)


def setup_inputs(seed: int = 0) -> dict:
    splits = jax.random.split(jax.random.key(seed), 10)
    ocean_state = noise(splits[0], (NLAT, NLON, C), 1.0, 6.0, ((0, 32), (1, 8)))
    kernel = noise(splits[1], (TAPS * TAPS, C), (TAPS * TAPS) ** -0.5, 0.875, (), jnp.float32)
    norm_gain = jnp.clip(jax.random.uniform(splits[2], (C,), jnp.float32, 0.5, 1.5), 0.5, 1.5)
    weight_in = noise(splits[3], (C, FF), C ** -0.5, 0.3125, ((0, 32),))
    weight_out = noise(splits[4], (FF, C), FF ** -0.5, 0.15625, ((0, 32),))
    layer_scale = jnp.clip(jax.random.uniform(splits[5], (C,), jnp.float32, 0.5, 1.5), 0.5, 1.5)
    cotangent = noise(splits[6], (NLAT, NLON, C), 1.0, 6.0, ((0, 32), (1, 8)))
    tile_list = draw_tile_list(jax.random.fold_in(splits[9], 71), 0)
    ocean_count = draw_ocean_count(jax.random.fold_in(splits[9], 71), 0)
    return {"ocean_state": ocean_state, "kernel": kernel, "norm_gain": norm_gain, "weight_in": weight_in, "weight_out": weight_out, "layer_scale": layer_scale, "cotangent": cotangent, "tile_list": tile_list, "ocean_count": ocean_count}


EPS = 1e-06
ROOT_HALF = 0.7071067811865476
INV_ROOT_TWO_PI = 0.3989422804014327

def gelu_value(hidden):
    return 0.5 * hidden * (1.0 + lax.erf(hidden * ROOT_HALF))

def gelu_slope(hidden):
    return 0.5 * (1.0 + lax.erf(hidden * ROOT_HALF)) + hidden * INV_ROOT_TWO_PI * jnp.exp(-0.5 * hidden * hidden)

def ocean_cells(tile_list, ocean_count):
    slot_ids = jnp.arange(tile_list.shape[-1], dtype=jnp.int32)
    live_slots = slot_ids < ocean_count[..., None]
    tile_ids = jnp.arange(TILES_DEV, dtype=jnp.int32)
    matches = (tile_list[..., None] == tile_ids) & live_slots[..., None]
    return jnp.any(matches, axis=-2).astype(jnp.float32)

def stencil(padded, kernel, height, breadth, flipped):
    summed = jnp.zeros((height, breadth, padded.shape[-1]), jnp.float32)
    for row_tap in range(TAPS):
        for col_tap in range(TAPS):
            if flipped:
                row_from = 2 * REACH - row_tap
                col_from = 2 * REACH - col_tap
            else:
                row_from = row_tap
                col_from = col_tap
            window = padded[row_from:row_from + height, col_from:col_from + breadth]
            summed = summed + kernel[row_tap * TAPS + col_tap] * window.astype(jnp.float32)
    return summed

def kernel_terms(padded, grad_conv, height, breadth):
    rows_out = []
    for row_tap in range(TAPS):
        for col_tap in range(TAPS):
            window = padded[row_tap:row_tap + height, col_tap:col_tap + breadth].astype(jnp.float32)
            rows_out.append(lax.optimization_barrier(jnp.sum(window * grad_conv, axis=(0, 1))))
    return jnp.stack(rows_out)

def wrap_pad(block):
    wrapped = jnp.concatenate([block[:, -REACH:], block, block[:, :REACH]], axis=1)
    zero_rows = jnp.zeros((REACH,) + wrapped.shape[1:], wrapped.dtype)
    return jnp.concatenate([zero_rows, wrapped, zero_rows], axis=0)

def pointwise(conv_rows, cot_rows, live_rows, norm_gain, layer_scale, weight_in, weight_out):
    centre = conv_rows - lax.optimization_barrier(jnp.mean(conv_rows, axis=-1, keepdims=True))
    spread = lax.rsqrt(lax.optimization_barrier(jnp.mean(centre * centre, axis=-1, keepdims=True)) + EPS)
    unit_rows = centre * spread
    normed = (unit_rows * norm_gain).astype(jnp.bfloat16)
    hidden = jnp.dot(normed, weight_in, preferred_element_type=jnp.float32)
    active = gelu_value(hidden).astype(jnp.bfloat16)
    mixed_rows = jnp.dot(active, weight_out, preferred_element_type=jnp.float32)
    grad_mixed = (live_rows * layer_scale * cot_rows.astype(jnp.float32)).astype(jnp.bfloat16)
    part_out = jnp.dot(active.T, grad_mixed, preferred_element_type=jnp.float32)
    grad_active = jnp.dot(grad_mixed, weight_out.T, preferred_element_type=jnp.float32)
    grad_hidden = (grad_active * gelu_slope(hidden)).astype(jnp.bfloat16)
    part_in = jnp.dot(normed.T, grad_hidden, preferred_element_type=jnp.float32)
    grad_normed = jnp.dot(grad_hidden, weight_in.T, preferred_element_type=jnp.float32)
    grad_unit = grad_normed * norm_gain
    grad_conv = spread * (grad_unit - lax.optimization_barrier(jnp.mean(grad_unit, axis=-1, keepdims=True)) - unit_rows * lax.optimization_barrier(jnp.mean(grad_unit * unit_rows, axis=-1, keepdims=True)))
    return (mixed_rows, grad_conv, part_in, part_out)

def reference(ocean_state, kernel, norm_gain, weight_in, weight_out, layer_scale, cotangent, tile_list, ocean_count):
    channels = ocean_state.shape[2]
    flags = ocean_cells(tile_list, ocean_count).reshape(LAT_DEVS, LON_DEVS, ROWS_DEV, TILES_ROW)
    flags = jnp.repeat(flags, TILE, axis=3)
    cell_mask = jnp.transpose(flags, (0, 2, 1, 3)).reshape(NLAT, NLON)
    extended = wrap_pad(ocean_state)

    def one_band(sums, band_id):
        sum_in, sum_out, sum_kernel = sums
        begin_row = band_id * ROWS_DEV
        window_rows = lax.dynamic_slice_in_dim(extended, begin_row, ROWS_DEV + 2 * REACH, 0)
        conv_field = stencil(window_rows, kernel, ROWS_DEV, NLON, False)
        live_rows = lax.dynamic_slice_in_dim(cell_mask, begin_row, ROWS_DEV, 0).reshape(-1, 1)
        cot_rows = lax.dynamic_slice_in_dim(cotangent, begin_row, ROWS_DEV, 0).reshape(-1, channels)
        state_rows = lax.dynamic_slice_in_dim(ocean_state, begin_row, ROWS_DEV, 0).reshape(-1, channels)
        mixed_rows, grad_conv, part_in, part_out = pointwise(conv_field.reshape(-1, channels), cot_rows, live_rows, norm_gain, layer_scale, weight_in, weight_out)
        new_rows = (state_rows.astype(jnp.float32) + live_rows * layer_scale * mixed_rows).astype(jnp.bfloat16)
        grad_conv = grad_conv.reshape(ROWS_DEV, NLON, channels)
        part_kernel = kernel_terms(window_rows, grad_conv, ROWS_DEV, NLON)
        sums = (sum_in + part_in, sum_out + part_out, sum_kernel + part_kernel)
        return (sums, (new_rows.reshape(ROWS_DEV, NLON, channels), grad_conv.astype(jnp.bfloat16)))
    start_sums = (jnp.zeros((channels, FF), jnp.float32), jnp.zeros((FF, channels), jnp.float32), jnp.zeros((TAPS * TAPS, channels), jnp.float32))
    band_ids = jnp.arange(NLAT // ROWS_DEV, dtype=jnp.int32)
    sums, (new_state, grad_half) = lax.scan(one_band, start_sums, band_ids)
    new_state = new_state.reshape(NLAT, NLON, channels)
    back_field = wrap_pad(grad_half.reshape(NLAT, NLON, channels))

    def adjoint_band(unused, band_id):
        begin_row = band_id * ROWS_DEV
        window_rows = lax.dynamic_slice_in_dim(back_field, begin_row, ROWS_DEV + 2 * REACH, 0)
        spread_back = stencil(window_rows, kernel, ROWS_DEV, NLON, True)
        cot_rows = lax.dynamic_slice_in_dim(cotangent, begin_row, ROWS_DEV, 0)
        return (unused, (cot_rows.astype(jnp.float32) + spread_back).astype(jnp.bfloat16))
    unused, grad_state = lax.scan(adjoint_band, None, band_ids)
    grad_state = grad_state.reshape(NLAT, NLON, channels)
    norm_factor = 1.0 / math.sqrt(NLAT * NLON)
    return (new_state, grad_state, sums[0] * norm_factor, sums[1] * norm_factor, sums[2] * norm_factor)
```

```python
import functools
import math

import jax
import jax.numpy as jnp
from jax import lax
from jax.experimental import pallas as pl
from jax.experimental.pallas import tpu as pltpu
from jax.sharding import PartitionSpec as P

TAPS = 7
REACH = 3
ROWS = 8
COLS = 128
C = 384
FF = 1536
NZ = 8
NY = 4
NX = 4
EPS = 1e-06
ROOT_HALF = 0.7071067811865476
INV_ROOT_TWO_PI = 0.3989422804014327
BF = jnp.bfloat16
F32 = jnp.float32
MESH = pl.DeviceIdType.MESH
N_SEM = 128


def gelu_pair(h):
    cdf = 0.5 * (1.0 + lax.erf(h * ROOT_HALF))
    return h * cdf, cdf + h * (INV_ROOT_TWO_PI * jnp.exp(-0.5 * h * h))


def nt(left, right):
    return lax.dot_general(left, right, (((1,), (1,)), ((), ())), preferred_element_type=F32)


def tn(left, right):
    return lax.dot_general(left, right, (((0,), (0,)), ((), ())), preferred_element_type=F32)


def nn(left, right):
    return jnp.dot(left, right, preferred_element_type=F32)


class Copy:
    def __init__(self, sems, src, dst, dev, land=None, send_if=None, recv_if=None):
        send, recv, counter = sems
        self.slot = counter[0]
        counter[0] += 1
        self.send_sem, self.recv_sem = send.at[self.slot], recv.at[self.slot]
        self.src, self.dst, self.dev = src, dst, dev
        self.land = dst if land is None else land
        self.send_if, self.recv_if = send_if, recv_if

    def _make(self, dst):
        return pltpu.make_async_remote_copy(
            src_ref=self.src,
            dst_ref=dst,
            send_sem=self.send_sem,
            recv_sem=self.recv_sem,
            device_id=self.dev,
            device_id_type=MESH,
        )

    def start(self):
        if self.send_if is None:
            self._make(self.dst).start()
        else:
            pl.when(self.send_if)(lambda: self._make(self.dst).start())

    def arrived(self):
        if self.recv_if is None:
            self._make(self.land).wait_recv()
        else:
            pl.when(self.recv_if)(lambda: self._make(self.land).wait_recv())

    def left(self):
        if self.send_if is None:
            self._make(self.dst).wait_send()
        else:
            pl.when(self.send_if)(lambda: self._make(self.dst).wait_send())


def kernel_body(
    tile_ref, count_ref, x_ref, k_ref, gain_ref, win_ref, wout_ref, scale_ref, cot_ref,
    new_ref, gs_ref, gwi_ref, gwo_ref, gk_ref,
    hrow, hcol, hcor, ext, ext2, k8, conv, spread_b, normed, npt, gm, ghalf,
    gath, w_in, sel, act, slope, gh, mixed, gn,
    ro, ri, cpo, cpi, ypo, ypi, xpo, xpi, xro, xri, zpo, zpi, zro, zri, fo, fi,
    kp, kz, kc, kx, ky, kcs, kxs, kys, kf,
    send, recv,
):
    lat, lon = lax.axis_index("lat"), lax.axis_index("lon")
    core, z, xlo = lax.rem(lat, 2), lax.rem(lat // 2, NZ), lat // (2 * NZ)
    y, xhi = lax.rem(lon, NY), lon // NY
    x = xhi * 2 + xlo
    q = xlo * NZ + z
    sems = (send, recv, [0])

    def at(xx, zz, cc, yy):
        return ((lax.rem(xx, 2) * NZ + zz) * 2 + cc, (xx // 2) * NY + yy)

    def ring(v, k, n):
        return lax.rem(v + k + n, n)

    def zdev(k):
        return at(x, ring(z, k, NZ), core, y)

    def xdev(k):
        return at(ring(x, k, NX), z, core, y)

    def ydev(k):
        return at(x, z, core, ring(y, k, NY))

    other_core = at(x, z, 1 - core, y)

    def around(dr, dc):
        return (ring(lat, dr, 32), ring(lon, dc, 8))

    barrier = pltpu.get_barrier_semaphore()
    partners = [around(dr, dc) for dr in (-1, 0, 1) for dc in (-1, 0, 1) if dr or dc]
    partners += [zdev(k) for k in range(1, NZ)]
    partners += [xdev(k) for k in range(1, NX)]
    partners += [ydev(k) for k in range(1, NY)]
    partners += [other_core]
    for dev in partners:
        pl.semaphore_signal(barrier, inc=1, device_id=dev, device_id_type=MESH)

    gath[lat, 0:64, :] = jnp.zeros((64, C), BF)
    for j in range(4):
        gath[lat, 16 * j : 16 * j + 12, :] = win_ref[:, C * j : C * (j + 1)]
    gath[lat, 64:112, :] = wout_ref[...]
    pl.semaphore_wait(barrier, len(partners))

    started = []

    def begin(copies):
        for c in copies:
            c.start()
            started.append(c)

    def halo_copies(src, n):
        top, bottom = pl.ds(0, REACH), pl.ds(ROWS - REACH, REACH)
        first, last, every = pl.ds(0, 16), pl.ds(COLS - 16, 16), pl.ds(0, ROWS)
        out = [
            Copy(sems, src.at[bottom], hrow.at[n, 0], around(1, 0)),
            Copy(sems, src.at[top], hrow.at[n, 1], around(-1, 0)),
            Copy(sems, src.at[every, last], hcol.at[n, 0], around(0, 1)),
            Copy(sems, src.at[every, first], hcol.at[n, 1], around(0, -1)),
            Copy(sems, src.at[bottom, last], hcor.at[n, 0], around(1, 1)),
            Copy(sems, src.at[bottom, first], hcor.at[n, 1], around(1, -1)),
            Copy(sems, src.at[top, last], hcor.at[n, 2], around(-1, 1)),
            Copy(sems, src.at[top, first], hcor.at[n, 3], around(-1, -1)),
        ]
        return out

    halo1 = halo_copies(x_ref, 0)
    begin(halo1)

    def shard(xl, zz, cc):
        return (xl * NZ + zz) * 2 + cc

    offsets = [0, -1, 1, -2, 2, -3, 3, -4]
    olo = 1 - xlo
    zc = {}
    for o in offsets[1:]:
        s = shard(xlo, ring(z, o, NZ), core)
        step = 1 if o < 0 else -1
        hop = shard(xlo, ring(z, o + step, NZ), core)
        zc[o] = Copy(sems, gath.at[hop], gath.at[hop], zdev(step), land=gath.at[s])
    xc, cc1, cc2 = {}, {}, {}
    for i, o in enumerate(offsets):
        s = shard(xlo, ring(z, o, NZ), core)
        so = shard(olo, ring(z, o, NZ), core)
        xc[o] = Copy(sems, gath.at[s], gath.at[s], xdev(1 if i % 2 == 0 else -1), land=gath.at[so])
        cc1[o] = Copy(
            sems, gath.at[s], gath.at[s], other_core, land=gath.at[shard(xlo, ring(z, o, NZ), 1 - core)]
        )
        cc2[o] = Copy(
            sems, gath.at[so], gath.at[so], other_core, land=gath.at[shard(olo, ring(z, o, NZ), 1 - core)]
        )

    begin([zc[-1], zc[1], xc[0], cc1[0]])

    def ring_step(n):
        for o in (-n, n):
            if o not in zc:
                continue
            zc[o].arrived()
            onward = o - 1 if o < 0 else o + 1
            go = [zc[onward]] if onward in zc else []
            begin(go + [xc[o], cc1[o]])

    def cross_step(n):
        for o in (-n, n) if n else (0,):
            if o in xc:
                xc[o].arrived()
                begin([cc2[o]])

    flags = []
    for r in range(ROWS):
        hit = jnp.int32(0)
        for s in range(6):
            match = jnp.logical_and(tile_ref[0, 0, s] == r, s < count_ref[0, 0])
            hit = hit + jnp.where(match, 1, 0)
        flags.append(hit.astype(F32))
    for l in range(3):
        for t in range(TAPS * TAPS):
            k8[l, t] = jnp.broadcast_to(k_ref[t : t + 1, 128 * l : 128 * (l + 1)], (8, 128))
    gain = gain_ref[...]
    scale = scale_ref[...]
    for r in range(ROWS):
        row_scale = scale * flags[r]
        gm[pl.ds(COLS * r, COLS), :] = (row_scale * cot_ref[r].astype(F32)).astype(BF)

    def lanes(l):
        return pl.ds(pl.multiple_of(l * 128, 128), 128)

    def extend(src, n, dst):
        up_on = jnp.where(lat > 0, 1.0, 0.0).astype(F32)
        down_on = jnp.where(lat < 31, 1.0, 0.0).astype(F32)

        def put(row, mid, left, right, on):
            for l in range(3):
                sl = slice(128 * l, 128 * (l + 1))
                m, a, b = mid[:, sl].astype(F32), left[:, sl].astype(F32), right[:, sl].astype(F32)
                if on is not None:
                    m, a, b = m * on, a * on, b * on
                dst[l, row, 8 : 8 + COLS, :] = m
                dst[l, row, 0:8, :] = a[8:16]
                dst[l, row, 8 + COLS : 16 + COLS, :] = b[0:8]

        def middle(r, carry):
            put(REACH + r, src[r], hcol[n, 0, r], hcol[n, 1, r], None)
            return carry

        def above(r, carry):
            put(r, hrow[n, 0, r], hcor[n, 0, r], hcor[n, 1, r], up_on)
            return carry

        def below(r, carry):
            put(REACH + ROWS + r, hrow[n, 1, r], hcor[n, 2, r], hcor[n, 3, r], down_on)
            return carry

        lax.fori_loop(0, ROWS, middle, 0)
        lax.fori_loop(0, REACH, above, 0)
        lax.fori_loop(0, REACH, below, 0)

    def stencil(src, flipped, emit, first, last):
        def body(i, carry):
            l, cg = i // 16, lax.rem(i, 16)
            c0 = pl.multiple_of(cg * 8, 8)
            acc = [None] * ROWS
            for b in range(TAPS):
                rows = [src[l, row, pl.ds(c0 + 5 + b, 8), :] for row in range(ROWS + 2 * REACH)]
                for a in range(TAPS):
                    t = a * TAPS + b
                    tap = k8[l, TAPS * TAPS - 1 - t if flipped else t]
                    for r in range(ROWS):
                        term = tap * rows[r + a]
                        acc[r] = term if acc[r] is None else acc[r] + term
            for r in range(ROWS):
                emit(r, pl.ds(c0, 8), lanes(l), acc[r])
            return carry

        lax.fori_loop(first, last, body, 0)

    for c in halo1:
        c.arrived()
    extend(x_ref, 0, ext)
    ring_step(1)

    def emit_conv(r, cs, ls, v):
        conv[r, cs, ls] = v

    stencil(ext, False, emit_conv, 0, 16)
    ring_step(2)
    cross_step(0)
    stencil(ext, False, emit_conv, 16, 32)
    ring_step(3)
    cross_step(1)
    stencil(ext, False, emit_conv, 32, 48)
    ring_step(4)
    cross_step(2)

    def norm_row(r, carry):
        v = conv[r]
        centre = v - jnp.mean(v, axis=-1, keepdims=True)
        sp = lax.rsqrt(jnp.mean(centre * centre, axis=-1, keepdims=True) + EPS)
        unit = centre * sp
        conv[r] = unit
        spread_b[r] = jnp.broadcast_to(sp, (COLS, 128))
        normed[pl.ds(pl.multiple_of(r * COLS, COLS), COLS), :] = (unit * gain).astype(BF)
        return carry

    lax.fori_loop(0, ROWS, norm_row, 0)
    cross_step(3)
    cross_step(4)

    m = lax.broadcasted_iota(jnp.int32, (512, C), 0)
    ch = lax.broadcasted_iota(jnp.int32, (512, C), 1)
    blk, inside = lax.shift_right_logical(m, 4), jnp.bitwise_and(m, 15)
    src_shard = 2 * jnp.bitwise_and(blk, 15) + lax.shift_right_logical(blk, 4)
    pick = jnp.logical_and(inside < 12, ch == 12 * src_shard + inside)
    sel[...] = jnp.where(pick, 1.0, 0.0).astype(BF)

    def spread_t(i, carry):
        cells = pl.ds(pl.multiple_of(i * 256, 256), 256)
        npt[:, cells] = nt(sel[...], normed[cells, :]).astype(BF)
        return carry

    lax.fori_loop(0, 4, spread_t, 0)

    m2 = lax.broadcasted_iota(jnp.int32, (C, 512), 1)
    ch2 = lax.broadcasted_iota(jnp.int32, (C, 512), 0)
    in2 = jnp.bitwise_and(m2, 15)
    pick2 = jnp.logical_and(in2 < 12, ch2 == 12 * lax.shift_right_logical(m2, 4) + in2)
    sel2 = jnp.where(pick2, 1.0, 0.0).astype(BF)

    for o in offsets:
        cc1[o].arrived()
        cc2[o].arrived()
    for j in range(4):
        w_in[j] = nn(sel2, gath[:, 16 * j : 16 * j + 16, :].reshape(512, C)).astype(BF)

    for j in range(4):
        wo = gath[8 * j : 8 * j + 8, 64:112, :].reshape(C, C)

        def forward(i, carry, j=j, wo=wo):
            cells = pl.ds(pl.multiple_of(i * 256, 256), 256)
            h = nn(normed[cells, :], w_in[j])
            value, grad = gelu_pair(h)
            value = value.astype(BF)
            act[cells, :] = value
            slope[j, cells, :] = grad
            mix = nn(value, wo)
            if j:
                mixed[cells, :] += mix
            else:
                mixed[cells, :] = mix
            return carry

        lax.fori_loop(0, 4, forward, 0)
        part = tn(act[...], gm[...]).astype(BF)
        for u in range(8):
            for i in range(3):
                ro[u % 2, i, 4 * j + u // 2] = part[48 * u + 16 * i : 48 * u + 16 * i + 16]

    has_out = y < 3

    class Reduction:
        def __init__(self, whole, cp, yp, xp, xr, zp, zr, f, uneven):
            self.__dict__.update(locals())
            pieces = 3 if uneven else 4
            on = has_out if uneven else None
            keep = pl.ds(0, pieces)
            self.on = on
            self.c = [Copy(sems, whole.at[1 - core, keep], cp.at[keep], other_core)]
            self.y, self.g = [], []
            for k in range(1, NY):
                yy, ys = ring(y, k, NY), ring(y, -k, NY)
                self.y.append(
                    Copy(
                        sems, cp.at[yy], yp.at[k - 1], ydev(k),
                        send_if=yy < 3 if uneven else None, recv_if=on,
                    )
                )
                self.g.append(
                    Copy(
                        sems, f.at[y], f.at[y], ydev(k), land=f.at[ys],
                        send_if=on, recv_if=ys < 3 if uneven else None,
                    )
                )
            self.x = []
            for k in range(1, NX):
                xx = ring(x, k, NX)
                self.x.append(
                    Copy(
                        sems, xp.at[pl.ds(lax.rem(xx, 2) * NZ, NZ)], xr.at[k - 1], xdev(k),
                        send_if=on, recv_if=on,
                    )
                )
            self.z = [
                Copy(sems, zp.at[ring(z, k, NZ)], zr.at[k - 1], zdev(k), send_if=on, recv_if=on)
                for k in range(1, NZ)
            ]
            self.pieces = pieces

        def when(self, fn):
            if self.on is None:
                fn()
            else:
                pl.when(self.on)(fn)

        def go_core(self):
            begin(self.c)

        def go_y(self):
            self.c[0].arrived()

            def add(i, carry):
                for n in range(self.pieces):
                    a = self.whole[core, n, i].astype(F32) + self.cp[n, i].astype(F32)
                    self.cp[n, i] = a.astype(BF)
                return carry

            lax.fori_loop(0, 16, add, 0)
            begin(self.y)

        def go_x(self):
            for c in self.y:
                c.arrived()

            def fn():
                def add(i, carry):
                    a = self.cp[y, i].astype(F32)
                    for n in range(3):
                        a = a + self.yp[n, i].astype(F32)
                    self.xp[i] = a.astype(BF)
                    return carry

                lax.fori_loop(0, 16, add, 0)

            self.when(fn)
            begin(self.x)

        def go_z(self):
            for c in self.x:
                c.arrived()

            def fn():
                def add(i, carry):
                    a = self.xp[xlo * NZ + i].astype(F32)
                    for n in range(3):
                        a = a + self.xr[n, i].astype(F32)
                    self.zp[i] = a.astype(BF)
                    return carry

                lax.fori_loop(0, NZ, add, 0)

            self.when(fn)
            begin(self.z)

        def go_gather(self):
            for c in self.z:
                c.arrived()

            def fn():
                a = self.zp[z].astype(F32)
                for n in range(NZ - 1):
                    a = a + self.zr[n].astype(F32)
                self.f[y] = a * NORM

            self.when(fn)
            begin(self.g)

        def finish(self):
            for c in self.g:
                c.arrived()

    NORM = 1.0 / math.sqrt(256 * 1024)
    out_sum = Reduction(ro, cpo, ypo, xpo, xro, zpo, zro, fo, True)
    in_sum = Reduction(ri, cpi, ypi, xpi, xri, zpi, zri, fi, False)
    out_sum.go_core()

    for j in range(4):
        wo = gath[8 * j : 8 * j + 8, 64:112, :].reshape(C, C)

        def backward(i, carry, j=j, wo=wo):
            cells = pl.ds(pl.multiple_of(i * 256, 256), 256)
            ga = nt(gm[cells, :], wo)
            g = (ga * slope[j, cells, :]).astype(BF)
            gh[cells, :] = g
            back = nt(g, w_in[j])
            if j:
                gn[cells, :] += back
            else:
                gn[cells, :] = back
            return carry

        lax.fori_loop(0, 4, backward, 0)
        part = nn(npt[...], gh[...]).astype(BF)
        ri[:, j] = part.reshape(2, 16, 16, C)
        if j == 1:
            out_sum.go_y()
    in_sum.go_core()

    def norm_back(r, carry):
        cells = pl.ds(pl.multiple_of(r * COLS, COLS), COLS)
        unit = conv[r]
        g = gn[cells, :] * gain
        sp = spread_b[r]
        sp = jnp.concatenate([sp, sp, sp], axis=1)
        first = jnp.mean(g, axis=-1, keepdims=True)
        second = jnp.mean(g * unit, axis=-1, keepdims=True)
        gc = sp * (g - first - unit * second)
        gn[cells, :] = gc
        ghalf[r] = gc.astype(BF)
        return carry

    lax.fori_loop(0, ROWS, norm_back, 0)
    halo2 = halo_copies(ghalf, 1)
    begin(halo2)
    in_sum.go_y()
    out_sum.go_x()

    for r in range(ROWS):
        row_scale = scale * flags[r]
        cells = pl.ds(COLS * r, COLS)
        new_ref[r] = (x_ref[r].astype(F32) + row_scale * mixed[cells, :]).astype(BF)

    for t in range(TAPS * TAPS, 64):
        kp[t // 8, t % 8 : t % 8 + 1, :] = jnp.zeros((1, C), F32)

    def tap_sums(l, carry):
        for b in range(TAPS):
            def body(cg, acc, b=b):
                c0 = pl.multiple_of(cg * 8, 8)
                rows = [ext[l, row, pl.ds(c0 + 5 + b, 8), :] for row in range(ROWS + 2 * REACH)]
                acc = list(acc)
                for r in range(ROWS):
                    g = gn[pl.ds(c0 + COLS * r, 8), lanes(l)]
                    for a in range(TAPS):
                        acc[a] = acc[a] + g * rows[r + a]
                return tuple(acc)

            acc = lax.fori_loop(0, 16, body, (jnp.zeros((8, 128), F32),) * TAPS)
            for a in range(TAPS):
                t = a * TAPS + b
                kp[t // 8, t % 8 : t % 8 + 1, lanes(l)] = jnp.sum(acc[a], axis=0, keepdims=True)
        return carry

    lax.fori_loop(0, 1, tap_sums, 0)
    out_sum.go_z()
    lax.fori_loop(1, 2, tap_sums, 0)
    lax.fori_loop(2, 3, tap_sums, 0)

    kz_c = [Copy(sems, kp.at[ring(z, k, NZ)], kz.at[k - 1], zdev(k)) for k in range(1, NZ)]
    kc_c = [Copy(sems, kcs, kc, other_core)]
    kx_c = [Copy(sems, kxs, kx.at[k - 1], xdev(k)) for k in range(1, NX)]
    ky_c = [Copy(sems, kys, ky.at[k - 1], ydev(k)) for k in range(1, NY)]
    kf_c = [
        Copy(sems, kf.at[z], kf.at[z], zdev(k), land=kf.at[ring(z, -k, NZ)]) for k in range(1, NZ)
    ]
    begin(kz_c)
    for c in halo2:
        c.arrived()
    extend(ghalf, 1, ext2)

    def arrive_all(copies):
        for c in copies:
            c.arrived()

    def emit_back(r, cs, ls, v):
        gs_part[r, cs, ls] = v

    gs_part = conv
    arrive_all(kz_c)
    total = kp[z]
    for n in range(NZ - 1):
        total = total + kz[n]
    kcs[...] = total
    begin(kc_c)
    in_sum.go_x()
    out_sum.go_gather()
    stencil(ext2, True, emit_back, 0, 16)
    arrive_all(kc_c)
    kxs[...] = kcs[...] + kc[...]
    begin(kx_c)
    in_sum.go_z()
    stencil(ext2, True, emit_back, 16, 32)
    arrive_all(kx_c)
    kys[...] = kxs[...] + kx[0] + kx[1] + kx[2]
    begin(ky_c)
    in_sum.go_gather()
    stencil(ext2, True, emit_back, 32, 48)
    arrive_all(ky_c)
    kf[z] = (kys[...] + ky[0] + ky[1] + ky[2]) * NORM
    begin(kf_c)

    def finish_row(r, carry):
        gs_ref[r] = (cot_ref[r].astype(F32) + gs_part[r]).astype(BF)
        return carry

    lax.fori_loop(0, ROWS, finish_row, 0)
    out_sum.finish()
    for i in range(3):
        gwo_ref[16 * i : 16 * i + 16, :] = fo[i]
    in_sum.finish()
    for j in range(4):
        gwi_ref[:, C * j : C * (j + 1)] = fi[j, 0:12, :]
    arrive_all(kf_c)
    for n in range(6):
        gk_ref[8 * n : 8 * n + 8, :] = kf[n]
    gk_ref[48:49, :] = kf[6, 0:1, :]
    for c in started:
        c.left()


def per_device(
    ocean_state, kernel, norm_gain, weight_in, weight_out, layer_scale, cotangent, tile_list, ocean_count
):
    vmem = pl.BlockSpec(memory_space=pltpu.VMEM)
    smem = pl.BlockSpec(memory_space=pltpu.SMEM)
    V = pltpu.VMEM
    scratch = [
        V((2, 2, REACH, COLS, C), BF),
        V((2, 2, ROWS, 16, C), BF),
        V((2, 4, REACH, 16, C), BF),
        V((3, 14, 144, 128), F32),
        V((3, 14, 144, 128), F32),
        V((3, 49, 8, 128), F32),
        V((ROWS, COLS, C), F32),
        V((ROWS, COLS, 128), F32),
        V((ROWS * COLS, C), BF),
        V((512, ROWS * COLS), BF),
        V((ROWS * COLS, C), BF),
        V((ROWS, COLS, C), BF),
        V((32, 112, C), BF),
        V((4, C, C), BF),
        V((512, C), BF),
        V((ROWS * COLS, C), BF),
        V((4, ROWS * COLS, C), F32),
        V((ROWS * COLS, C), BF),
        V((ROWS * COLS, C), F32),
        V((ROWS * COLS, C), F32),
        V((2, 4, 16, 16, C), BF),
        V((2, 4, 16, 16, C), BF),
        V((4, 16, 16, C), BF),
        V((4, 16, 16, C), BF),
        V((3, 16, 16, C), BF),
        V((3, 16, 16, C), BF),
        V((16, 16, C), BF),
        V((16, 16, C), BF),
        V((3, NZ, 16, C), BF),
        V((3, NZ, 16, C), BF),
        V((NZ, 16, C), BF),
        V((NZ, 16, C), BF),
        V((NZ - 1, 16, C), BF),
        V((NZ - 1, 16, C), BF),
        V((4, 16, C), F32),
        V((4, 16, C), F32),
        V((NZ, 8, C), F32),
        V((NZ - 1, 8, C), F32),
        V((8, C), F32),
        V((3, 8, C), F32),
        V((3, 8, C), F32),
        V((8, C), F32),
        V((8, C), F32),
        V((8, C), F32),
        V((NZ, 8, C), F32),
        pltpu.SemaphoreType.DMA((N_SEM,)),
        pltpu.SemaphoreType.DMA((N_SEM,)),
    ]
    return pl.pallas_call(
        kernel_body,
        out_shape=(
            jax.ShapeDtypeStruct((ROWS, COLS, C), BF),
            jax.ShapeDtypeStruct((ROWS, COLS, C), BF),
            jax.ShapeDtypeStruct((12, FF), F32),
            jax.ShapeDtypeStruct((48, C), F32),
            jax.ShapeDtypeStruct((TAPS * TAPS, C), F32),
        ),
        in_specs=[smem, smem] + [vmem] * 7,
        out_specs=(vmem,) * 5,
        scratch_shapes=scratch,
        compiler_params=pltpu.CompilerParams(
            collective_id=0, has_side_effects=True, vmem_limit_bytes=60 * 2**20
        ),
        cost_estimate=pl.CostEstimate(
            flops=8 * 10**9, bytes_accessed=4 * 10**6, transcendentals=4 * 10**6
        ),
        name="block",
    )(
        tile_list, ocean_count, ocean_state, kernel, norm_gain.reshape(1, C), weight_in, weight_out,
        layer_scale.reshape(1, C), cotangent,
    )


def solution(mesh):
    return jax.shard_map(
        per_device,
        mesh=mesh,
        in_specs=(
            P("lat", "lon", None),
            P(),
            P(),
            P("lat", None),
            P("lat", None),
            P(),
            P("lat", "lon", None),
            P("lat", "lon", None),
            P("lat", "lon"),
        ),
        out_specs=(
            P("lat", "lon", None),
            P("lat", "lon", None),
            P("lat", None),
            P("lat", None),
            P(),
        ),
        check_vma=False,
    )
```

```python
import functools
import math

import jax
import jax.numpy as jnp
from jax import lax
from jax.experimental import pallas as pl
from jax.experimental.pallas import tpu as pltpu
from jax.sharding import PartitionSpec as P

TAPS = 7
REACH = 3
ROWS = 8
COLS = 128
C = 384
FF = 1536
NZ = 8
NY = 4
NX = 4
EPS = 1e-06
ROOT_HALF = 0.7071067811865476
INV_ROOT_TWO_PI = 0.3989422804014327
BF = jnp.bfloat16
F32 = jnp.float32
MESH = pl.DeviceIdType.MESH
N_SEM = 192
HALVES = 2
HALF = FF // HALVES


def gelu_pair(h):
    cdf = 0.5 * (1.0 + lax.erf(h * ROOT_HALF))
    return h * cdf, cdf + h * (INV_ROOT_TWO_PI * jnp.exp(-0.5 * h * h))


def nt(left, right):
    return lax.dot_general(left, right, (((1,), (1,)), ((), ())), preferred_element_type=F32)


def tn(left, right):
    return lax.dot_general(left, right, (((0,), (0,)), ((), ())), preferred_element_type=F32)


def nn(left, right):
    return jnp.dot(left, right, preferred_element_type=F32)


class Copy:
    def __init__(self, sems, src, dst, dev, land=None, send_if=None, recv_if=None):
        send, recv, counter = sems
        self.slot = counter[0]
        counter[0] += 1
        self.send_sem, self.recv_sem = send.at[self.slot], recv.at[self.slot]
        self.src, self.dst, self.dev = src, dst, dev
        self.land = dst if land is None else land
        self.send_if, self.recv_if = send_if, recv_if

    def _make(self, dst):
        return pltpu.make_async_remote_copy(
            src_ref=self.src,
            dst_ref=dst,
            send_sem=self.send_sem,
            recv_sem=self.recv_sem,
            device_id=self.dev,
            device_id_type=MESH,
        )

    def start(self):
        if self.send_if is None:
            self._make(self.dst).start()
        else:
            pl.when(self.send_if)(lambda: self._make(self.dst).start())

    def arrived(self):
        if self.recv_if is None:
            self._make(self.land).wait_recv()
        else:
            pl.when(self.recv_if)(lambda: self._make(self.land).wait_recv())

    def left(self):
        if self.send_if is None:
            self._make(self.dst).wait_send()
        else:
            pl.when(self.send_if)(lambda: self._make(self.dst).wait_send())


def kernel_body(
    tile_ref, count_ref, x_ref, k_ref, gain_ref, win_ref, wout_ref, scale_ref, cot_ref,
    new_ref, gs_ref, gwi_ref, gwo_ref, gk_ref,
    hrow, hcol, hcor, ext, ext2, k8, conv, spread_b, normed, npt, gm, ghalf,
    pack, gin, gout, unpack, w_in, sel, act, slope, gh, mixed, gn,
    ro, ri, cpo, cpi, ypo, ypi, xpo, xpi, xro, xri, zpo, zpi, zro, zri, fo, fi,
    kp, kz, kc, kx, ky, kcs, kxs, kys, kf,
    send, recv,
):
    lat, lon = lax.axis_index("lat"), lax.axis_index("lon")
    core, z, xlo = lax.rem(lat, 2), lax.rem(lat // 2, NZ), lat // (2 * NZ)
    y, xhi = lax.rem(lon, NY), lon // NY
    x = xhi * 2 + xlo
    q = xlo * NZ + z
    sems = (send, recv, [0])

    def at(xx, zz, cc, yy):
        return ((lax.rem(xx, 2) * NZ + zz) * 2 + cc, (xx // 2) * NY + yy)

    def ring(v, k, n):
        return lax.rem(v + k + n, n)

    def zdev(k):
        return at(x, ring(z, k, NZ), core, y)

    def xdev(k):
        return at(ring(x, k, NX), z, core, y)

    def ydev(k):
        return at(x, z, core, ring(y, k, NY))

    other_core = at(x, z, 1 - core, y)

    def around(dr, dc):
        return (ring(lat, dr, 32), ring(lon, dc, 8))

    barrier = pltpu.get_barrier_semaphore()
    partners = [around(dr, dc) for dr in (-1, 0, 1) for dc in (-1, 0, 1) if dr or dc]
    partners += [zdev(k) for k in range(1, NZ)]
    partners += [xdev(k) for k in range(1, NX)]
    partners += [ydev(k) for k in range(1, NY)]
    partners += [other_core]
    for dev in partners:
        pl.semaphore_signal(barrier, inc=1, device_id=dev, device_id_type=MESH)

    for b in range(3):
        pack[b, 0:12, :] = win_ref[:, C * b : C * (b + 1)].astype(F32)
        pack[b, 12:16, :] = win_ref[4 * b : 4 * b + 4, 3 * C : 4 * C].astype(F32)
        gin[lat, b] = pack[b].astype(BF)
    gout[lat] = wout_ref[...]
    pl.semaphore_wait(barrier, len(partners))

    started = []

    def begin(copies):
        for c in copies:
            c.start()
            started.append(c)

    def halo_copies(src, n):
        top, bottom = pl.ds(0, REACH), pl.ds(ROWS - REACH, REACH)
        first, last, every = pl.ds(0, 16), pl.ds(COLS - 16, 16), pl.ds(0, ROWS)
        out = [
            Copy(sems, src.at[bottom], hrow.at[n, 0], around(1, 0)),
            Copy(sems, src.at[top], hrow.at[n, 1], around(-1, 0)),
            Copy(sems, src.at[every, last], hcol.at[n, 0], around(0, 1)),
            Copy(sems, src.at[every, first], hcol.at[n, 1], around(0, -1)),
            Copy(sems, src.at[bottom, last], hcor.at[n, 0], around(1, 1)),
            Copy(sems, src.at[bottom, first], hcor.at[n, 1], around(1, -1)),
            Copy(sems, src.at[top, last], hcor.at[n, 2], around(-1, 1)),
            Copy(sems, src.at[top, first], hcor.at[n, 3], around(-1, -1)),
        ]
        return out

    halo1 = halo_copies(x_ref, 0)
    begin(halo1)

    def shard(xl, zz, cc):
        return (xl * NZ + zz) * 2 + cc

    order = [1, 7, 2, 6, 3, 5, 4]
    olo = 1 - xlo

    class Gather:
        def __init__(self, buf):
            self.z, self.x, self.c1, self.c2 = {}, {}, {}, {}
            mine = buf.at[lat]
            for i, k in enumerate([0] + order):
                zz = ring(z, -k, NZ)
                s, so = shard(xlo, zz, core), shard(olo, zz, core)
                far, faro = shard(xlo, zz, 1 - core), shard(olo, zz, 1 - core)
                if k:
                    self.z[k] = Copy(sems, mine, mine, zdev(k), land=buf.at[s])
                self.x[k] = Copy(
                    sems, buf.at[s], buf.at[s], xdev(1 if i % 2 == 0 else -1), land=buf.at[so]
                )
                self.c1[k] = Copy(sems, buf.at[s], buf.at[s], other_core, land=buf.at[far])
                self.c2[k] = Copy(sems, buf.at[so], buf.at[so], other_core, land=buf.at[faro])

        def launch(self):
            begin([self.z[k] for k in order] + [self.x[0], self.c1[0]])

        def onward(self, *ks):
            for k in ks:
                self.z[k].arrived()
                begin([self.x[k], self.c1[k]])

        def across(self, *ks):
            for k in ks:
                self.x[k].arrived()
                begin([self.c2[k]])

        def done(self):
            for k in [0] + order:
                self.c1[k].arrived()
                self.c2[k].arrived()

    gather_in, gather_out = Gather(gin), Gather(gout)
    gather_in.launch()

    flags = []
    for r in range(ROWS):
        hit = jnp.int32(0)
        for s in range(6):
            match = jnp.logical_and(tile_ref[0, 0, s] == r, s < count_ref[0, 0])
            hit = hit + jnp.where(match, 1, 0)
        flags.append(hit.astype(F32))
    for l in range(3):
        for t in range(TAPS * TAPS):
            k8[l, t] = jnp.broadcast_to(k_ref[t : t + 1, 128 * l : 128 * (l + 1)], (8, 128))
    gain = gain_ref[...].reshape(1, C)
    scale = scale_ref[...].reshape(1, C)
    for r in range(ROWS):
        row_scale = scale * flags[r]
        gm[pl.ds(COLS * r, COLS), :] = (row_scale * cot_ref[r].astype(F32)).astype(BF)

    def lanes(l):
        return pl.ds(pl.multiple_of(l * 128, 128), 128)

    def put_row(dst, row, mid, on):
        for l in range(3):
            m = mid[:, 128 * l : 128 * (l + 1)].astype(F32)
            dst[l, row, 8 : 8 + COLS, :] = m if on is None else m * on

    def put_sides(dst, row, left, right, on):
        for l in range(3):
            sl = slice(128 * l, 128 * (l + 1))
            a, b = left[:, sl].astype(F32), right[:, sl].astype(F32)
            if on is not None:
                a, b = a * on, b * on
            dst[l, row, 0:8, :] = a[8:16]
            dst[l, row, 8 + COLS : 16 + COLS, :] = b[0:8]

    def extend_own(src, dst):
        def middle(r, carry):
            put_row(dst, REACH + r, src[r], None)
            return carry

        lax.fori_loop(0, ROWS, middle, 0)

    def extend_rim(n, dst):
        up_on = jnp.where(lat > 0, 1.0, 0.0).astype(F32)
        down_on = jnp.where(lat < 31, 1.0, 0.0).astype(F32)

        def middle(r, carry):
            put_sides(dst, REACH + r, hcol[n, 0, r], hcol[n, 1, r], None)
            return carry

        def outer(r, carry):
            put_row(dst, r, hrow[n, 0, r], up_on)
            put_sides(dst, r, hcor[n, 0, r], hcor[n, 1, r], up_on)
            put_row(dst, REACH + ROWS + r, hrow[n, 1, r], down_on)
            put_sides(dst, REACH + ROWS + r, hcor[n, 2, r], hcor[n, 3, r], down_on)
            return carry

        lax.fori_loop(0, ROWS, middle, 0)
        lax.fori_loop(0, REACH, outer, 0)

    own_rows = tuple(range(REACH, REACH + ROWS))
    rim_rows = tuple(range(REACH)) + tuple(range(REACH + ROWS, 2 * REACH + ROWS))

    def tile_sums(src, flipped, l, c0, rows_in, acc):
        for b in range(TAPS):
            rows = {row: src[l, row, pl.ds(c0 + 5 + b, 8), :] for row in rows_in}
            for a in range(TAPS):
                t = a * TAPS + b
                tap = k8[l, TAPS * TAPS - 1 - t if flipped else t]
                for r in range(ROWS):
                    if r + a in rows:
                        term = tap * rows[r + a]
                        acc[r] = term if acc[r] is None else acc[r] + term
        return acc

    def stencil(src, flipped, out, first, last):
        def body(i, carry):
            l, c0 = i // 16, pl.multiple_of(lax.rem(i, 16) * 8, 8)
            acc = tile_sums(src, flipped, l, c0, own_rows + rim_rows, [None] * ROWS)
            for r in range(ROWS):
                out[r, pl.ds(c0, 8), lanes(l)] = acc[r]
            return carry

        lax.fori_loop(first, last, body, 0)

    def stencil_own(src, out, first, last):
        def body(i, carry):
            l, c0 = i // 14, pl.multiple_of(lax.rem(i, 14) * 8 + 8, 8)
            acc = tile_sums(src, False, l, c0, own_rows, [None] * ROWS)
            for r in range(ROWS):
                out[r, pl.ds(c0, 8), lanes(l)] = acc[r]
            return carry

        lax.fori_loop(first, last, body, 0)

    def stencil_rim(src, out):
        touched = (0, 1, 2, 5, 6, 7)

        def body(i, carry):
            l, c0 = i // 14, pl.multiple_of(lax.rem(i, 14) * 8 + 8, 8)
            acc = [out[r, pl.ds(c0, 8), lanes(l)] if r in touched else None for r in range(ROWS)]
            acc = tile_sums(src, False, l, c0, rim_rows, acc)
            for r in touched:
                out[r, pl.ds(c0, 8), lanes(l)] = acc[r]
            return carry

        def sides(i, carry):
            l, c0 = i // 2, pl.multiple_of(lax.rem(i, 2) * 120, 8)
            acc = tile_sums(src, False, l, c0, own_rows + rim_rows, [None] * ROWS)
            for r in range(ROWS):
                out[r, pl.ds(c0, 8), lanes(l)] = acc[r]
            return carry

        lax.fori_loop(0, 42, body, 0)
        lax.fori_loop(0, 6, sides, 0)

    extend_own(x_ref, ext)
    stencil_own(ext, conv, 0, 42)
    gather_in.onward(1, 7)
    gather_out.launch()
    for c in halo1:
        c.arrived()
    extend_rim(0, ext)
    gather_in.onward(2, 6)
    gather_in.across(0)
    stencil_rim(ext, conv)
    gather_in.onward(3, 5)
    gather_in.across(1, 7)

    def norm_row(r, carry):
        v = conv[r]
        centre = v - jnp.mean(v, axis=-1, keepdims=True)
        sp = lax.rsqrt(jnp.mean(centre * centre, axis=-1, keepdims=True) + EPS)
        unit = centre * sp
        conv[r] = unit
        spread_b[r] = jnp.broadcast_to(sp, (COLS, 128))
        normed[pl.ds(pl.multiple_of(r * COLS, COLS), COLS), :] = (unit * gain).astype(BF)
        return carry

    lax.fori_loop(0, ROWS, norm_row, 0)
    gather_in.onward(4)
    gather_in.across(2, 6)
    gather_out.onward(1, 7)

    m = lax.broadcasted_iota(jnp.int32, (C, C), 0)
    ch = lax.broadcasted_iota(jnp.int32, (C, C), 1)
    half = jnp.where(m >= 192, 1, 0)
    u = m - 192 * half
    inside = u - 12 * lax.shift_right_logical(u * 5462, 16)
    sel[...] = jnp.where(ch == 2 * u - inside + 12 * half, 1.0, 0.0).astype(BF)
    npt[...] = nt(sel[...], normed[...]).astype(BF)

    m2 = lax.broadcasted_iota(jnp.int32, (C, 512), 1)
    ch2 = lax.broadcasted_iota(jnp.int32, (C, 512), 0)
    in2 = jnp.bitwise_and(m2, 15)
    at2 = 12 * lax.shift_right_logical(m2, 4) + in2
    for b in range(3):
        top = jnp.logical_and(in2 < 12, ch2 == at2)
        low = jnp.logical_and(in2 >= 12, ch2 == at2 + 4 * b - 12)
        unpack[0] = jnp.where(top, 1.0, 0.0).astype(BF)
        unpack[1 + b] = jnp.where(low, 1.0, 0.0).astype(BF)
    gather_in.across(3, 5, 4)
    gather_out.onward(2, 6)
    gather_out.across(0, 1, 7)
    gather_in.done()
    rest = None
    for b in range(3):
        g = gin[:, b].reshape(512, C)
        w_in[b // 2, :, C * (b % 2) : C * (b % 2 + 1)] = nn(unpack[0], g).astype(BF)
        low = nn(unpack[1 + b], g)
        rest = low if b == 0 else rest + low
    w_in[1, :, C:] = rest.astype(BF)

    for j in range(HALVES):
        h = nn(normed[...], w_in[j])
        value, grad = gelu_pair(h)
        act[j] = value.astype(BF)
        slope[j] = grad
        if j == 0:
            gather_out.onward(3, 5, 4)
            gather_out.across(2, 6)
    gather_out.across(3, 5, 4)
    gather_out.done()
    for j in range(HALVES):
        part = tn(act[j], gm[...]).astype(BF)
        for u in range(16):
            q_to = 8 * j + u // 2
            for i in range(3):
                ro[u % 2, i, 16 * q_to : 16 * q_to + 16] = part[48 * u + 16 * i : 48 * u + 16 * i + 16]

    has_out = y < 3

    class Reduction:
        def __init__(self, whole, cp, yp, xp, xr, zp, zr, f, uneven):
            self.__dict__.update(locals())
            on = has_out if uneven else None
            self.on = on
            self.pieces = 3 if uneven else 4
            self.rows = whole.shape[2]
            self.part = self.rows // 2
            self.c = [Copy(sems, whole.at[1 - core], cp, other_core)]
            self.y, self.g = [], []
            for k in range(1, NY):
                yy, ys = ring(y, k, NY), ring(y, -k, NY)
                last = self.pieces - 1
                self.y.append(
                    Copy(
                        sems, cp.at[jnp.minimum(yy, last)], yp.at[k - 1], ydev(k),
                        send_if=yy < 3 if uneven else None, recv_if=on,
                    )
                )
                self.g.append(
                    Copy(
                        sems, f.at[jnp.minimum(y, last)], f.at[jnp.minimum(y, last)], ydev(k),
                        land=f.at[jnp.minimum(ys, last)],
                        send_if=on, recv_if=ys < 3 if uneven else None,
                    )
                )
            self.x = []
            for k in range(1, NX):
                xx = ring(x, k, NX)
                self.x.append(
                    Copy(
                        sems, xp.at[self.side(lax.rem(xx, 2))], xr.at[k - 1], xdev(k),
                        send_if=on, recv_if=on,
                    )
                )
            self.z = [
                Copy(sems, zp.at[ring(z, k, NZ)], zr.at[k - 1], zdev(k), send_if=on, recv_if=on)
                for k in range(1, NZ)
            ]

        def side(self, lo):
            return pl.ds(pl.multiple_of(lo * self.part, 16), self.part)

        def when(self, fn):
            if self.on is None:
                fn()
            else:
                pl.when(self.on)(fn)

        def go_core(self):
            begin(self.c)

        def go_y(self):
            self.c[0].arrived()

            def add(i, carry):
                rows = pl.ds(pl.multiple_of(i * 64, 16), 64)
                for n in range(self.pieces):
                    a = self.whole[core, n, rows].astype(F32) + self.cp[n, rows].astype(F32)
                    self.cp[n, rows] = a.astype(BF)
                return carry

            lax.fori_loop(0, self.rows // 64, add, 0)
            begin(self.y)

        def go_x(self):
            for c in self.y:
                c.arrived()

            def fn():
                own = jnp.minimum(y, self.pieces - 1)

                def add(i, carry):
                    rows = pl.ds(pl.multiple_of(i * 64, 16), 64)
                    a = self.cp[own, rows].astype(F32)
                    for n in range(3):
                        a = a + self.yp[n, rows].astype(F32)
                    self.xp[rows] = a.astype(BF)
                    return carry

                lax.fori_loop(0, self.rows // 64, add, 0)

            self.when(fn)
            begin(self.x)

        def go_z(self):
            for c in self.x:
                c.arrived()

            def fn():
                a = self.xp[self.side(xlo)].astype(F32)
                for n in range(3):
                    a = a + self.xr[n].astype(F32)
                a = a.astype(BF)
                if self.part != NZ * 16:
                    to = lax.broadcasted_iota(jnp.int32, (NZ * 16, self.part), 0)
                    fr = lax.broadcasted_iota(jnp.int32, (NZ * 16, self.part), 1)
                    slot = jnp.bitwise_and(to, 15)
                    pick = jnp.logical_and(
                        slot < 12, fr == 12 * lax.shift_right_logical(to, 4) + slot
                    )
                    a = nn(jnp.where(pick, 1.0, 0.0).astype(BF), a).astype(BF)
                self.zp[...] = a.reshape(NZ, 16, C)

            self.when(fn)
            begin(self.z)

        def go_gather(self):
            for c in self.z:
                c.arrived()

            def fn():
                a = self.zp[z].astype(F32)
                for n in range(NZ - 1):
                    a = a + self.zr[n].astype(F32)
                self.f[jnp.minimum(y, self.pieces - 1)] = a * NORM

            self.when(fn)
            begin(self.g)

        def finish(self):
            for c in self.g:
                c.arrived()

    NORM = 1.0 / math.sqrt(256 * 1024)
    out_sum = Reduction(ro, cpo, ypo, xpo, xro, zpo, zro, fo, True)
    in_sum = Reduction(ri, cpi, ypi, xpi, xri, zpi, zri, fi, False)
    out_sum.go_core()

    for j in range(HALVES):
        wo = gout[16 * j : 16 * j + 16].reshape(HALF, C)
        ga = nn(gm[...], wo.T)
        gh[j] = (ga * slope[j]).astype(BF)
        part = nn(npt[...], gh[j]).astype(BF)
        for n in range(2):
            for c in range(2):
                ri[c, 2 * j + n] = part[192 * c : 192 * c + 192, C * n : C * (n + 1)]
        if j == 0:
            out_sum.go_y()
    in_sum.go_core()
    gn[...] = nn(gh[0], w_in[0].T) + nn(gh[1], w_in[1].T)
    in_sum.go_y()

    def norm_back(r, carry):
        cells = pl.ds(pl.multiple_of(r * COLS, COLS), COLS)
        unit = conv[r]
        g = gn[cells, :] * gain
        sp = spread_b[r]
        sp = jnp.concatenate([sp, sp, sp], axis=1)
        first = jnp.mean(g, axis=-1, keepdims=True)
        second = jnp.mean(g * unit, axis=-1, keepdims=True)
        gc = sp * (g - first - unit * second)
        gn[cells, :] = gc
        ghalf[r] = gc.astype(BF)
        return carry

    lax.fori_loop(0, ROWS, norm_back, 0)
    halo2 = halo_copies(ghalf, 1)
    begin(halo2)

    for t in range(TAPS * TAPS, 64):
        kp[t // 8, t % 8 : t % 8 + 1, :] = jnp.zeros((1, C), F32)

    def tap_sums(l, carry):
        for b in range(TAPS):
            def body(cg, acc, b=b):
                c0 = pl.multiple_of(cg * 8, 8)
                rows = [ext[l, row, pl.ds(c0 + 5 + b, 8), :] for row in range(ROWS + 2 * REACH)]
                acc = list(acc)
                for r in range(ROWS):
                    g = gn[pl.ds(c0 + COLS * r, 8), lanes(l)]
                    for a in range(TAPS):
                        acc[a] = acc[a] + g * rows[r + a]
                return tuple(acc)

            acc = lax.fori_loop(0, 16, body, (jnp.zeros((8, 128), F32),) * TAPS)
            for a in range(TAPS):
                t = a * TAPS + b
                kp[t // 8, t % 8 : t % 8 + 1, lanes(l)] = jnp.sum(acc[a], axis=0, keepdims=True)
        return carry

    lax.fori_loop(0, 2, tap_sums, 0)
    out_sum.go_x()
    lax.fori_loop(2, 3, tap_sums, 0)

    kz_c = [Copy(sems, kp.at[ring(z, k, NZ)], kz.at[k - 1], zdev(k)) for k in range(1, NZ)]
    kc_c = [Copy(sems, kcs, kc, other_core)]
    kx_c = [Copy(sems, kxs, kx.at[k - 1], xdev(k)) for k in range(1, NX)]
    ky_c = [Copy(sems, kys, ky.at[k - 1], ydev(k)) for k in range(1, NY)]
    kf_c = [
        Copy(sems, kf.at[z], kf.at[z], zdev(k), land=kf.at[ring(z, -k, NZ)]) for k in range(1, NZ)
    ]
    def arrive_all(copies):
        for c in copies:
            c.arrived()

    begin(kz_c)
    extend_own(ghalf, ext2)
    mixed[...] = nn(act[0], gout[0:16].reshape(HALF, C)) + nn(act[1], gout[16:32].reshape(HALF, C))
    for r in range(ROWS):
        row_scale = scale * flags[r]
        cells = pl.ds(COLS * r, COLS)
        new_ref[r] = (x_ref[r].astype(F32) + row_scale * mixed[cells, :]).astype(BF)
    arrive_all(halo2)
    extend_rim(1, ext2)
    in_sum.go_x()

    gs_part = conv
    stencil(ext2, True, gs_part, 0, 16)
    arrive_all(kz_c)
    total = kp[z]
    for n in range(NZ - 1):
        total = total + kz[n]
    kcs[...] = total
    begin(kc_c)
    out_sum.go_z()
    stencil(ext2, True, gs_part, 16, 24)
    arrive_all(kc_c)
    kxs[...] = kcs[...] + kc[...]
    begin(kx_c)
    stencil(ext2, True, gs_part, 24, 36)
    in_sum.go_z()
    stencil(ext2, True, gs_part, 36, 40)
    arrive_all(kx_c)
    kys[...] = kxs[...] + kx[0] + kx[1] + kx[2]
    begin(ky_c)
    stencil(ext2, True, gs_part, 40, 48)
    out_sum.go_gather()
    arrive_all(ky_c)
    kf[z] = (kys[...] + ky[0] + ky[1] + ky[2]) * NORM
    begin(kf_c)
    in_sum.go_gather()

    def finish_row(r, carry):
        gs_ref[r] = (cot_ref[r].astype(F32) + gs_part[r]).astype(BF)
        return carry

    lax.fori_loop(0, ROWS, finish_row, 0)
    out_sum.finish()
    for i in range(3):
        gwo_ref[16 * i : 16 * i + 16, :] = fo[i]
    in_sum.finish()
    for j in range(4):
        gwi_ref[:, C * j : C * (j + 1)] = fi[j, 0:12, :]
    arrive_all(kf_c)
    for n in range(6):
        gk_ref[8 * n : 8 * n + 8, :] = kf[n]
    gk_ref[48:49, :] = kf[6, 0:1, :]
    for c in started:
        c.left()


def per_device(
    ocean_state, kernel, norm_gain, weight_in, weight_out, layer_scale, cotangent, tile_list, ocean_count
):
    vmem = pl.BlockSpec(memory_space=pltpu.VMEM)
    smem = pl.BlockSpec(memory_space=pltpu.SMEM)
    V = pltpu.VMEM
    scratch = [
        V((2, 2, REACH, COLS, C), BF),
        V((2, 2, ROWS, 16, C), BF),
        V((2, 4, REACH, 16, C), BF),
        V((3, 14, 144, 128), F32),
        V((3, 14, 144, 128), F32),
        V((3, 49, 8, 128), F32),
        V((ROWS, COLS, C), F32),
        V((ROWS, COLS, 128), F32),
        V((ROWS * COLS, C), BF),
        V((C, ROWS * COLS), BF),
        V((ROWS * COLS, C), BF),
        V((ROWS, COLS, C), BF),
        V((3, 16, C), F32),
        V((32, 3, 16, C), BF),
        V((32, 48, C), BF),
        V((4, C, 512), BF),
        V((HALVES, C, HALF), BF),
        V((C, C), BF),
        V((HALVES, ROWS * COLS, HALF), BF),
        V((HALVES, ROWS * COLS, HALF), F32),
        V((HALVES, ROWS * COLS, HALF), BF),
        V((ROWS * COLS, C), F32),
        V((ROWS * COLS, C), F32),
        V((2, 3, 256, C), BF),
        V((2, 4, 192, C), BF),
        V((3, 256, C), BF),
        V((4, 192, C), BF),
        V((3, 256, C), BF),
        V((3, 192, C), BF),
        V((256, C), BF),
        V((192, C), BF),
        V((3, 128, C), BF),
        V((3, 96, C), BF),
        V((NZ, 16, C), BF),
        V((NZ, 16, C), BF),
        V((NZ - 1, 16, C), BF),
        V((NZ - 1, 16, C), BF),
        V((3, 16, C), F32),
        V((4, 16, C), F32),
        V((NZ, 8, C), F32),
        V((NZ - 1, 8, C), F32),
        V((8, C), F32),
        V((3, 8, C), F32),
        V((3, 8, C), F32),
        V((8, C), F32),
        V((8, C), F32),
        V((8, C), F32),
        V((NZ, 8, C), F32),
        pltpu.SemaphoreType.DMA((N_SEM,)),
        pltpu.SemaphoreType.DMA((N_SEM,)),
    ]
    return pl.pallas_call(
        kernel_body,
        out_shape=(
            jax.ShapeDtypeStruct((ROWS, COLS, C), BF),
            jax.ShapeDtypeStruct((ROWS, COLS, C), BF),
            jax.ShapeDtypeStruct((12, FF), F32),
            jax.ShapeDtypeStruct((48, C), F32),
            jax.ShapeDtypeStruct((TAPS * TAPS, C), F32),
        ),
        in_specs=[smem, smem] + [vmem] * 7,
        out_specs=(vmem,) * 5,
        scratch_shapes=scratch,
        compiler_params=pltpu.CompilerParams(
            collective_id=0, has_side_effects=True, vmem_limit_bytes=60 * 2**20
        ),
        cost_estimate=pl.CostEstimate(
            flops=8 * 10**9, bytes_accessed=4 * 10**6, transcendentals=4 * 10**6
        ),
        name="block",
    )(
        tile_list, ocean_count, ocean_state, kernel, norm_gain, weight_in, weight_out,
        layer_scale, cotangent,
    )


def solution(mesh):
    return jax.shard_map(
        per_device,
        mesh=mesh,
        in_specs=(
            P("lat", "lon", None),
            P(),
            P(),
            P("lat", None),
            P("lat", None),
            P(),
            P("lat", "lon", None),
            P("lat", "lon", None),
            P("lat", "lon"),
        ),
        out_specs=(
            P("lat", "lon", None),
            P("lat", "lon", None),
            P("lat", None),
            P("lat", None),
            P(),
        ),
        check_vma=False,
    )
```

```python
import functools
import math

import jax
import jax.numpy as jnp
from jax import lax
from jax.experimental import pallas as pl
from jax.experimental.pallas import tpu as pltpu
from jax.sharding import PartitionSpec as P

TAPS = 7
REACH = 3
ROWS = 8
COLS = 128
C = 384
FF = 1536
NZ = 8
NY = 4
NX = 4
EPS = 1e-06
ROOT_HALF = 0.7071067811865476
INV_ROOT_TWO_PI = 0.3989422804014327
BF = jnp.bfloat16
F32 = jnp.float32
MESH = pl.DeviceIdType.MESH
N_SEM = 192
HALVES = 2
HALF = FF // HALVES


def gelu_pair(h):
    cdf = 0.5 * (1.0 + lax.erf(h * ROOT_HALF))
    return h * cdf, cdf + h * (INV_ROOT_TWO_PI * jnp.exp(-0.5 * h * h))


def nt(left, right):
    return lax.dot_general(left, right, (((1,), (1,)), ((), ())), preferred_element_type=F32)


def tn(left, right):
    return lax.dot_general(left, right, (((0,), (0,)), ((), ())), preferred_element_type=F32)


def nn(left, right):
    return jnp.dot(left, right, preferred_element_type=F32)


class Copy:
    def __init__(self, sems, src, dst, dev, land=None, send_if=None, recv_if=None):
        send, recv, counter = sems
        self.slot = counter[0]
        counter[0] += 1
        self.send_sem, self.recv_sem = send.at[self.slot], recv.at[self.slot]
        self.src, self.dst, self.dev = src, dst, dev
        self.land = dst if land is None else land
        self.send_if, self.recv_if = send_if, recv_if

    def _make(self, dst):
        return pltpu.make_async_remote_copy(
            src_ref=self.src,
            dst_ref=dst,
            send_sem=self.send_sem,
            recv_sem=self.recv_sem,
            device_id=self.dev,
            device_id_type=MESH,
        )

    def start(self):
        if self.send_if is None:
            self._make(self.dst).start()
        else:
            pl.when(self.send_if)(lambda: self._make(self.dst).start())

    def arrived(self):
        if self.recv_if is None:
            self._make(self.land).wait_recv()
        else:
            pl.when(self.recv_if)(lambda: self._make(self.land).wait_recv())

    def left(self):
        if self.send_if is None:
            self._make(self.dst).wait_send()
        else:
            pl.when(self.send_if)(lambda: self._make(self.dst).wait_send())


def kernel_body(
    tile_ref, count_ref, x_ref, k_ref, gain_ref, win_ref, wout_ref, scale_ref, cot_ref,
    new_ref, gs_ref, gwi_ref, gwo_ref, gk_ref,
    hrow, hcol, hcor, ext, ext2, k8, conv, spread_b, normed, npt, gm, ghalf,
    pack, gin, gout, unpack, w_in, sel, act, slope, gh, mixed, gn,
    ro, ri, cpo, cpi, ypo, ypi, xpo, xpi, xro, xri, zpo, zpi, zro, zri, fo, fi,
    kp, kz, kc, kxy, kcs, kcs2, kf,
    send, recv,
):
    lat, lon = lax.axis_index("lat"), lax.axis_index("lon")
    core, z, xlo = lax.rem(lat, 2), lax.rem(lat // 2, NZ), lat // (2 * NZ)
    y, xhi = lax.rem(lon, NY), lon // NY
    x = xhi * 2 + xlo
    q = xlo * NZ + z
    sems = (send, recv, [0])

    def at(xx, zz, cc, yy):
        return ((lax.rem(xx, 2) * NZ + zz) * 2 + cc, (xx // 2) * NY + yy)

    def ring(v, k, n):
        return lax.rem(v + k + n, n)

    def zdev(k):
        return at(x, ring(z, k, NZ), core, y)

    def xdev(k):
        return at(ring(x, k, NX), z, core, y)

    def ydev(k):
        return at(x, z, core, ring(y, k, NY))

    other_core = at(x, z, 1 - core, y)

    def plane(i, j):
        return at(ring(x, i, NX), z, core, ring(y, j, NY))

    def around(dr, dc):
        return (ring(lat, dr, 32), ring(lon, dc, 8))

    barrier = pltpu.get_barrier_semaphore()
    partners = [around(dr, dc) for dr in (-1, 0, 1) for dc in (-1, 0, 1) if dr or dc]
    partners += [zdev(k) for k in range(1, NZ)]
    partners += [xdev(k) for k in range(1, NX)]
    partners += [ydev(k) for k in range(1, NY)]
    partners += [other_core]
    partners += [plane(i, j) for i in range(1, NX) for j in range(1, NY)]
    for dev in partners:
        pl.semaphore_signal(barrier, inc=1, device_id=dev, device_id_type=MESH)

    for b in range(3):
        pack[b, 0:12, :] = win_ref[:, C * b : C * (b + 1)].astype(F32)
        pack[b, 12:16, :] = win_ref[4 * b : 4 * b + 4, 3 * C : 4 * C].astype(F32)
        gin[lat, b] = pack[b].astype(BF)
    gout[lat] = wout_ref[...]
    pl.semaphore_wait(barrier, len(partners))

    started = []

    def begin(copies):
        for c in copies:
            c.start()
            started.append(c)

    def halo_copies(src, n):
        top, bottom = pl.ds(0, REACH), pl.ds(ROWS - REACH, REACH)
        first, last, every = pl.ds(0, 16), pl.ds(COLS - 16, 16), pl.ds(0, ROWS)
        out = [
            Copy(sems, src.at[bottom], hrow.at[n, 0], around(1, 0)),
            Copy(sems, src.at[top], hrow.at[n, 1], around(-1, 0)),
            Copy(sems, src.at[every, last], hcol.at[n, 0], around(0, 1)),
            Copy(sems, src.at[every, first], hcol.at[n, 1], around(0, -1)),
            Copy(sems, src.at[bottom, last], hcor.at[n, 0], around(1, 1)),
            Copy(sems, src.at[bottom, first], hcor.at[n, 1], around(1, -1)),
            Copy(sems, src.at[top, last], hcor.at[n, 2], around(-1, 1)),
            Copy(sems, src.at[top, first], hcor.at[n, 3], around(-1, -1)),
        ]
        return out

    halo1 = halo_copies(x_ref, 0)
    begin(halo1)

    def shard(xl, zz, cc):
        return (xl * NZ + zz) * 2 + cc

    order = [1, 7, 2, 6, 3, 5, 4]
    olo = 1 - xlo

    class Gather:
        def __init__(self, buf):
            self.z, self.x, self.c1, self.c2 = {}, {}, {}, {}
            mine = buf.at[lat]
            for i, k in enumerate([0] + order):
                zz = ring(z, -k, NZ)
                s, so = shard(xlo, zz, core), shard(olo, zz, core)
                far, faro = shard(xlo, zz, 1 - core), shard(olo, zz, 1 - core)
                if k:
                    self.z[k] = Copy(sems, mine, mine, zdev(k), land=buf.at[s])
                self.x[k] = Copy(
                    sems, buf.at[s], buf.at[s], xdev(1 if i % 2 == 0 else -1), land=buf.at[so]
                )
                self.c1[k] = Copy(sems, buf.at[s], buf.at[s], other_core, land=buf.at[far])
                self.c2[k] = Copy(sems, buf.at[so], buf.at[so], other_core, land=buf.at[faro])

        def launch(self):
            begin([self.z[k] for k in order] + [self.x[0], self.c1[0]])

        def onward(self, *ks):
            for k in ks:
                self.z[k].arrived()
                begin([self.x[k], self.c1[k]])

        def across(self, *ks):
            for k in ks:
                self.x[k].arrived()
                begin([self.c2[k]])

        def done(self):
            for k in [0] + order:
                self.c1[k].arrived()
                self.c2[k].arrived()

    gather_in, gather_out = Gather(gin), Gather(gout)
    gather_in.launch()

    flags = []
    for r in range(ROWS):
        hit = jnp.int32(0)
        for s in range(6):
            match = jnp.logical_and(tile_ref[0, 0, s] == r, s < count_ref[0, 0])
            hit = hit + jnp.where(match, 1, 0)
        flags.append(hit.astype(F32))
    for l in range(3):
        for t in range(TAPS * TAPS):
            k8[l, t] = jnp.broadcast_to(k_ref[t : t + 1, 128 * l : 128 * (l + 1)], (8, 128))
    gain = gain_ref[...].reshape(1, C)
    scale = scale_ref[...].reshape(1, C)
    for r in range(ROWS):
        row_scale = scale * flags[r]
        gm[pl.ds(COLS * r, COLS), :] = (row_scale * cot_ref[r].astype(F32)).astype(BF)

    def lanes(l):
        return pl.ds(pl.multiple_of(l * 128, 128), 128)

    def put_row(dst, row, mid, on):
        for l in range(3):
            m = mid[:, 128 * l : 128 * (l + 1)].astype(F32)
            dst[l, row, 8 : 8 + COLS, :] = m if on is None else m * on

    def put_sides(dst, row, left, right, on):
        for l in range(3):
            sl = slice(128 * l, 128 * (l + 1))
            a, b = left[:, sl].astype(F32), right[:, sl].astype(F32)
            if on is not None:
                a, b = a * on, b * on
            dst[l, row, 0:8, :] = a[8:16]
            dst[l, row, 8 + COLS : 16 + COLS, :] = b[0:8]

    def extend_own(src, dst):
        def middle(r, carry):
            put_row(dst, REACH + r, src[r], None)
            return carry

        lax.fori_loop(0, ROWS, middle, 0)

    def extend_rim(n, dst):
        up_on = jnp.where(lat > 0, 1.0, 0.0).astype(F32)
        down_on = jnp.where(lat < 31, 1.0, 0.0).astype(F32)

        def middle(r, carry):
            put_sides(dst, REACH + r, hcol[n, 0, r], hcol[n, 1, r], None)
            return carry

        def outer(r, carry):
            put_row(dst, r, hrow[n, 0, r], up_on)
            put_sides(dst, r, hcor[n, 0, r], hcor[n, 1, r], up_on)
            put_row(dst, REACH + ROWS + r, hrow[n, 1, r], down_on)
            put_sides(dst, REACH + ROWS + r, hcor[n, 2, r], hcor[n, 3, r], down_on)
            return carry

        lax.fori_loop(0, ROWS, middle, 0)
        lax.fori_loop(0, REACH, outer, 0)

    own_rows = tuple(range(REACH, REACH + ROWS))
    rim_rows = tuple(range(REACH)) + tuple(range(REACH + ROWS, 2 * REACH + ROWS))

    def tile_sums(src, flipped, l, c0, rows_in, acc):
        for b in range(TAPS):
            rows = {row: src[l, row, pl.ds(c0 + 5 + b, 8), :] for row in rows_in}
            for a in range(TAPS):
                t = a * TAPS + b
                tap = k8[l, TAPS * TAPS - 1 - t if flipped else t]
                for r in range(ROWS):
                    if r + a in rows:
                        term = tap * rows[r + a]
                        acc[r] = term if acc[r] is None else acc[r] + term
        return acc

    def stencil(src, flipped, out, first, last):
        def body(i, carry):
            l, c0 = i // 16, pl.multiple_of(lax.rem(i, 16) * 8, 8)
            acc = tile_sums(src, flipped, l, c0, own_rows + rim_rows, [None] * ROWS)
            for r in range(ROWS):
                out[r, pl.ds(c0, 8), lanes(l)] = acc[r]
            return carry

        lax.fori_loop(first, last, body, 0)

    def stencil_own(src, out, first, last):
        def body(i, carry):
            l, c0 = i // 14, pl.multiple_of(lax.rem(i, 14) * 8 + 8, 8)
            acc = tile_sums(src, False, l, c0, own_rows, [None] * ROWS)
            for r in range(ROWS):
                out[r, pl.ds(c0, 8), lanes(l)] = acc[r]
            return carry

        lax.fori_loop(first, last, body, 0)

    def stencil_rim(src, out):
        touched = (0, 1, 2, 5, 6, 7)

        def body(i, carry):
            l, c0 = i // 14, pl.multiple_of(lax.rem(i, 14) * 8 + 8, 8)
            acc = [out[r, pl.ds(c0, 8), lanes(l)] if r in touched else None for r in range(ROWS)]
            acc = tile_sums(src, False, l, c0, rim_rows, acc)
            for r in touched:
                out[r, pl.ds(c0, 8), lanes(l)] = acc[r]
            return carry

        def sides(i, carry):
            l, c0 = i // 2, pl.multiple_of(lax.rem(i, 2) * 120, 8)
            acc = tile_sums(src, False, l, c0, own_rows + rim_rows, [None] * ROWS)
            for r in range(ROWS):
                out[r, pl.ds(c0, 8), lanes(l)] = acc[r]
            return carry

        lax.fori_loop(0, 42, body, 0)
        lax.fori_loop(0, 6, sides, 0)

    extend_own(x_ref, ext)
    stencil_own(ext, conv, 0, 42)
    gather_in.onward(1, 7)
    for c in halo1:
        c.arrived()
    extend_rim(0, ext)
    gather_in.onward(2, 6)
    gather_in.across(0)
    gather_out.launch()
    stencil_rim(ext, conv)
    gather_in.onward(3, 5)
    gather_in.across(1, 7)

    def norm_row(r, carry):
        v = conv[r]
        centre = v - jnp.mean(v, axis=-1, keepdims=True)
        sp = lax.rsqrt(jnp.mean(centre * centre, axis=-1, keepdims=True) + EPS)
        unit = centre * sp
        conv[r] = unit
        spread_b[r] = jnp.broadcast_to(sp, (COLS, 128))
        normed[pl.ds(pl.multiple_of(r * COLS, COLS), COLS), :] = (unit * gain).astype(BF)
        return carry

    lax.fori_loop(0, ROWS, norm_row, 0)
    gather_in.onward(4)
    gather_in.across(2, 6)
    gather_out.onward(1, 7)

    m = lax.broadcasted_iota(jnp.int32, (C, C), 0)
    ch = lax.broadcasted_iota(jnp.int32, (C, C), 1)
    half = jnp.where(m >= 192, 1, 0)
    u = m - 192 * half
    inside = u - 12 * lax.shift_right_logical(u * 5462, 16)
    sel[...] = jnp.where(ch == 2 * u - inside + 12 * half, 1.0, 0.0).astype(BF)
    npt[...] = nt(sel[...], normed[...]).astype(BF)

    m2 = lax.broadcasted_iota(jnp.int32, (C, 512), 1)
    ch2 = lax.broadcasted_iota(jnp.int32, (C, 512), 0)
    in2 = jnp.bitwise_and(m2, 15)
    at2 = 12 * lax.shift_right_logical(m2, 4) + in2
    for b in range(3):
        top = jnp.logical_and(in2 < 12, ch2 == at2)
        low = jnp.logical_and(in2 >= 12, ch2 == at2 + 4 * b - 12)
        unpack[0] = jnp.where(top, 1.0, 0.0).astype(BF)
        unpack[1 + b] = jnp.where(low, 1.0, 0.0).astype(BF)
    gather_in.across(3, 5, 4)
    gather_out.onward(2, 6)
    gather_out.across(0, 1, 7)
    gather_in.done()
    rest = None
    for b in range(3):
        g = gin[:, b].reshape(512, C)
        w_in[b // 2, :, C * (b % 2) : C * (b % 2 + 1)] = nn(unpack[0], g).astype(BF)
        low = nn(unpack[1 + b], g)
        rest = low if b == 0 else rest + low
    w_in[1, :, C:] = rest.astype(BF)

    for j in range(HALVES):
        h = nn(normed[...], w_in[j])
        value, grad = gelu_pair(h)
        act[j] = value.astype(BF)
        slope[j] = grad
        if j == 0:
            gather_out.onward(3, 5, 4)
            gather_out.across(2, 6)
    gather_out.across(3, 5, 4)
    gather_out.done()
    for j in range(HALVES):
        part = tn(act[j], gm[...]).astype(BF)
        for u in range(16):
            q_to = 8 * j + u // 2
            for i in range(3):
                ro[u % 2, i, 16 * q_to : 16 * q_to + 16] = part[48 * u + 16 * i : 48 * u + 16 * i + 16]

    has_out = y < 3

    class Reduction:
        def __init__(self, whole, cp, yp, xp, xr, zp, zr, f, uneven):
            self.__dict__.update(locals())
            on = has_out if uneven else None
            self.on = on
            self.pieces = 3 if uneven else 4
            self.rows = whole.shape[2]
            self.part = self.rows // 2
            self.c = [Copy(sems, whole.at[1 - core], cp, other_core)]
            self.y, self.g = [], []
            for k in range(1, NY):
                yy, ys = ring(y, k, NY), ring(y, -k, NY)
                last = self.pieces - 1
                self.y.append(
                    Copy(
                        sems, cp.at[jnp.minimum(yy, last)], yp.at[k - 1], ydev(k),
                        send_if=yy < 3 if uneven else None, recv_if=on,
                    )
                )
                self.g.append(
                    Copy(
                        sems, f.at[jnp.minimum(y, last)], f.at[jnp.minimum(y, last)], ydev(k),
                        land=f.at[jnp.minimum(ys, last)],
                        send_if=on, recv_if=ys < 3 if uneven else None,
                    )
                )
            self.x = []
            for k in range(1, NX):
                xx = ring(x, k, NX)
                self.x.append(
                    Copy(
                        sems, xp.at[self.side(lax.rem(xx, 2))], xr.at[k - 1], xdev(k),
                        send_if=on, recv_if=on,
                    )
                )
            self.z = [
                Copy(sems, zp.at[ring(z, k, NZ)], zr.at[k - 1], zdev(k), send_if=on, recv_if=on)
                for k in range(1, NZ)
            ]

        def side(self, lo):
            return pl.ds(pl.multiple_of(lo * self.part, 16), self.part)

        def when(self, fn):
            if self.on is None:
                fn()
            else:
                pl.when(self.on)(fn)

        def go_core(self):
            begin(self.c)

        def go_y(self):
            self.c[0].arrived()

            def add(i, carry):
                rows = pl.ds(pl.multiple_of(i * 64, 16), 64)
                for n in range(self.pieces):
                    a = self.whole[core, n, rows].astype(F32) + self.cp[n, rows].astype(F32)
                    self.cp[n, rows] = a.astype(BF)
                return carry

            lax.fori_loop(0, self.rows // 64, add, 0)
            begin(self.y)

        def go_x(self):
            for c in self.y:
                c.arrived()

            def fn():
                own = jnp.minimum(y, self.pieces - 1)

                def add(i, carry):
                    rows = pl.ds(pl.multiple_of(i * 64, 16), 64)
                    a = self.cp[own, rows].astype(F32)
                    for n in range(3):
                        a = a + self.yp[n, rows].astype(F32)
                    self.xp[rows] = a.astype(BF)
                    return carry

                lax.fori_loop(0, self.rows // 64, add, 0)

            self.when(fn)
            begin(self.x)

        def go_z(self):
            for c in self.x:
                c.arrived()

            def fn():
                a = self.xp[self.side(xlo)].astype(F32)
                for n in range(3):
                    a = a + self.xr[n].astype(F32)
                a = a.astype(BF)
                if self.part != NZ * 16:
                    to = lax.broadcasted_iota(jnp.int32, (NZ * 16, self.part), 0)
                    fr = lax.broadcasted_iota(jnp.int32, (NZ * 16, self.part), 1)
                    slot = jnp.bitwise_and(to, 15)
                    pick = jnp.logical_and(
                        slot < 12, fr == 12 * lax.shift_right_logical(to, 4) + slot
                    )
                    a = nn(jnp.where(pick, 1.0, 0.0).astype(BF), a).astype(BF)
                self.zp[...] = a.reshape(NZ, 16, C)

            self.when(fn)
            begin(self.z)

        def go_gather(self):
            for c in self.z:
                c.arrived()

            def fn():
                a = self.zp[z].astype(F32)
                for n in range(NZ - 1):
                    a = a + self.zr[n].astype(F32)
                self.f[jnp.minimum(y, self.pieces - 1)] = a * NORM

            self.when(fn)
            begin(self.g)

        def finish(self):
            for c in self.g:
                c.arrived()

    NORM = 1.0 / math.sqrt(256 * 1024)
    out_sum = Reduction(ro, cpo, ypo, xpo, xro, zpo, zro, fo, True)
    in_sum = Reduction(ri, cpi, ypi, xpi, xri, zpi, zri, fi, False)
    out_sum.go_core()

    for j in range(HALVES):
        wo = gout[16 * j : 16 * j + 16].reshape(HALF, C)
        ga = nn(gm[...], wo.T)
        gh[j] = (ga * slope[j]).astype(BF)
        part = nn(npt[...], gh[j]).astype(BF)
        for n in range(2):
            for c in range(2):
                ri[c, 2 * j + n] = part[192 * c : 192 * c + 192, C * n : C * (n + 1)]
        if j == 0:
            out_sum.go_y()
    in_sum.go_core()
    gn[...] = nn(gh[0], w_in[0].T) + nn(gh[1], w_in[1].T)
    in_sum.go_y()

    def norm_back(r, carry):
        cells = pl.ds(pl.multiple_of(r * COLS, COLS), COLS)
        unit = conv[r]
        g = gn[cells, :] * gain
        sp = spread_b[r]
        sp = jnp.concatenate([sp, sp, sp], axis=1)
        first = jnp.mean(g, axis=-1, keepdims=True)
        second = jnp.mean(g * unit, axis=-1, keepdims=True)
        gc = sp * (g - first - unit * second)
        gn[cells, :] = gc
        ghalf[r] = gc.astype(BF)
        return carry

    lax.fori_loop(0, ROWS, norm_back, 0)
    halo2 = halo_copies(ghalf, 1)
    begin(halo2)

    for t in range(TAPS * TAPS, 64):
        kp[t // 8, t % 8 : t % 8 + 1, :] = jnp.zeros((1, C), F32)

    def tap_sums(l, carry):
        for b in range(TAPS):
            def body(cg, acc, b=b):
                c0 = pl.multiple_of(cg * 8, 8)
                rows = [ext[l, row, pl.ds(c0 + 5 + b, 8), :] for row in range(ROWS + 2 * REACH)]
                acc = list(acc)
                for r in range(ROWS):
                    g = gn[pl.ds(c0 + COLS * r, 8), lanes(l)]
                    for a in range(TAPS):
                        acc[a] = acc[a] + g * rows[r + a]
                return tuple(acc)

            acc = lax.fori_loop(0, 16, body, (jnp.zeros((8, 128), F32),) * TAPS)
            for a in range(TAPS):
                t = a * TAPS + b
                kp[t // 8, t % 8 : t % 8 + 1, lanes(l)] = jnp.sum(acc[a], axis=0, keepdims=True)
        return carry

    lax.fori_loop(0, 2, tap_sums, 0)
    out_sum.go_x()
    lax.fori_loop(2, 3, tap_sums, 0)

    kz_c = [Copy(sems, kp.at[ring(z, k, NZ)], kz.at[k - 1], zdev(k)) for k in range(1, NZ)]
    kc_c = [Copy(sems, kcs, kc, other_core)]
    steps = [(i, j) for i in range(NX) for j in range(NY) if i or j]
    kp_c = [Copy(sems, kcs2, kxy.at[n], plane(*d)) for n, d in enumerate(steps)]
    kf_c = [
        Copy(sems, kf.at[z], kf.at[z], zdev(k), land=kf.at[ring(z, -k, NZ)]) for k in range(1, NZ)
    ]
    def arrive_all(copies):
        for c in copies:
            c.arrived()

    begin(kz_c)
    extend_own(ghalf, ext2)
    mixed[...] = nn(act[0], gout[0:16].reshape(HALF, C)) + nn(act[1], gout[16:32].reshape(HALF, C))
    for r in range(ROWS):
        row_scale = scale * flags[r]
        cells = pl.ds(COLS * r, COLS)
        new_ref[r] = (x_ref[r].astype(F32) + row_scale * mixed[cells, :]).astype(BF)
    arrive_all(halo2)
    extend_rim(1, ext2)
    in_sum.go_x()

    gs_part = conv
    stencil(ext2, True, gs_part, 0, 16)
    arrive_all(kz_c)
    total = kp[z]
    for n in range(NZ - 1):
        total = total + kz[n]
    kcs[...] = total
    begin(kc_c)
    out_sum.go_z()
    stencil(ext2, True, gs_part, 16, 24)
    arrive_all(kc_c)
    kcs2[...] = kcs[...] + kc[...]
    begin(kp_c)
    stencil(ext2, True, gs_part, 24, 36)
    in_sum.go_z()
    stencil(ext2, True, gs_part, 36, 44)
    arrive_all(kp_c)
    total = kcs2[...]
    for n in range(NX * NY - 1):
        total = total + kxy[n]
    kf[z] = total * NORM
    begin(kf_c)
    out_sum.go_gather()
    stencil(ext2, True, gs_part, 44, 48)
    in_sum.go_gather()

    def finish_row(r, carry):
        gs_ref[r] = (cot_ref[r].astype(F32) + gs_part[r]).astype(BF)
        return carry

    lax.fori_loop(0, ROWS, finish_row, 0)
    out_sum.finish()
    for i in range(3):
        gwo_ref[16 * i : 16 * i + 16, :] = fo[i]
    in_sum.finish()
    for j in range(4):
        gwi_ref[:, C * j : C * (j + 1)] = fi[j, 0:12, :]
    arrive_all(kf_c)
    for n in range(6):
        gk_ref[8 * n : 8 * n + 8, :] = kf[n]
    gk_ref[48:49, :] = kf[6, 0:1, :]
    for c in started:
        c.left()


def per_device(
    ocean_state, kernel, norm_gain, weight_in, weight_out, layer_scale, cotangent, tile_list, ocean_count
):
    vmem = pl.BlockSpec(memory_space=pltpu.VMEM)
    smem = pl.BlockSpec(memory_space=pltpu.SMEM)
    V = pltpu.VMEM
    scratch = [
        V((2, 2, REACH, COLS, C), BF),
        V((2, 2, ROWS, 16, C), BF),
        V((2, 4, REACH, 16, C), BF),
        V((3, 14, 144, 128), F32),
        V((3, 14, 144, 128), F32),
        V((3, 49, 8, 128), F32),
        V((ROWS, COLS, C), F32),
        V((ROWS, COLS, 128), F32),
        V((ROWS * COLS, C), BF),
        V((C, ROWS * COLS), BF),
        V((ROWS * COLS, C), BF),
        V((ROWS, COLS, C), BF),
        V((3, 16, C), F32),
        V((32, 3, 16, C), BF),
        V((32, 48, C), BF),
        V((4, C, 512), BF),
        V((HALVES, C, HALF), BF),
        V((C, C), BF),
        V((HALVES, ROWS * COLS, HALF), BF),
        V((HALVES, ROWS * COLS, HALF), F32),
        V((HALVES, ROWS * COLS, HALF), BF),
        V((ROWS * COLS, C), F32),
        V((ROWS * COLS, C), F32),
        V((2, 3, 256, C), BF),
        V((2, 4, 192, C), BF),
        V((3, 256, C), BF),
        V((4, 192, C), BF),
        V((3, 256, C), BF),
        V((3, 192, C), BF),
        V((256, C), BF),
        V((192, C), BF),
        V((3, 128, C), BF),
        V((3, 96, C), BF),
        V((NZ, 16, C), BF),
        V((NZ, 16, C), BF),
        V((NZ - 1, 16, C), BF),
        V((NZ - 1, 16, C), BF),
        V((3, 16, C), F32),
        V((4, 16, C), F32),
        V((NZ, 8, C), F32),
        V((NZ - 1, 8, C), F32),
        V((8, C), F32),
        V((NX * NY - 1, 8, C), F32),
        V((8, C), F32),
        V((8, C), F32),
        V((NZ, 8, C), F32),
        pltpu.SemaphoreType.DMA((N_SEM,)),
        pltpu.SemaphoreType.DMA((N_SEM,)),
    ]
    return pl.pallas_call(
        kernel_body,
        out_shape=(
            jax.ShapeDtypeStruct((ROWS, COLS, C), BF),
            jax.ShapeDtypeStruct((ROWS, COLS, C), BF),
            jax.ShapeDtypeStruct((12, FF), F32),
            jax.ShapeDtypeStruct((48, C), F32),
            jax.ShapeDtypeStruct((TAPS * TAPS, C), F32),
        ),
        in_specs=[smem, smem] + [vmem] * 7,
        out_specs=(vmem,) * 5,
        scratch_shapes=scratch,
        compiler_params=pltpu.CompilerParams(
            collective_id=0, has_side_effects=True, vmem_limit_bytes=60 * 2**20
        ),
        cost_estimate=pl.CostEstimate(
            flops=8 * 10**9, bytes_accessed=4 * 10**6, transcendentals=4 * 10**6
        ),
        name="block",
    )(
        tile_list, ocean_count, ocean_state, kernel, norm_gain, weight_in, weight_out,
        layer_scale, cotangent,
    )


def solution(mesh):
    return jax.shard_map(
        per_device,
        mesh=mesh,
        in_specs=(
            P("lat", "lon", None),
            P(),
            P(),
            P("lat", None),
            P("lat", None),
            P(),
            P("lat", "lon", None),
            P("lat", "lon", None),
            P("lat", "lon"),
        ),
        out_specs=(
            P("lat", "lon", None),
            P("lat", "lon", None),
            P("lat", None),
            P("lat", None),
            P(),
        ),
        check_vma=False,
    )
```
